512 devices in a mesh: chan: 64 (over z, x, y_hi), rblk: 8 (over y_lo, core).
Axes of the slice: x: 4, y: 8 (y_hi: 2, y_lo: 4; y = y_hi * 4 + y_lo), z: 8, core: 2. Of those that a mesh axis runs over, the one named last changes fastest.
Arguments:
- records: bfloat16 [8, 5120, 7680], P(None, ('rblk', 'chan')), may hold values from -64 to 64
- source_index: int32 [64], replicated, may hold values from 0 to 5119, as said below
- band_edges: int32 [33], replicated, may hold values from 0 to 1536, as said below
Outputs:
- correlations: bfloat16 [1536, 2, 64, 5120], P('chan', None, None, 'rblk')
The draws below stay inside these ranges and needn't reach their ends.
Inputs may be any that keep to these rules, and one draw needn't show every extreme that they name: `source_index`: 64 distinct channel numbers. `band_edges`: begins with 0, ends with 1536, and rises by 32 or more at every step.
All inputs are finite; a program needn't handle non-finite values.
Results may differ from the reference program's by a relative error of at most 0.001.
Values sent between devices are 32-bit elements; how exact they have to be, the bound alone decides.
No kernel may reach another device: no remote copies, remote signals or barrier semaphores. Data moves between devices by JAX's collectives and lax.ppermute only.
A program may use at most 128 MiB of HBM per device.

```python
import jax
import jax.numpy as jnp
from jax import lax

SEG = 8
TP = 60
TQ = 128
F_LOW = 7
NF = 1536
NB = 32
BAND_MIN = 32
NS = 64
NCH = 5120


def draw_records(key, part):
    key = jax.random.fold_in(key, 11)
    noise_key, taps_key = jax.random.split(key, 2)
    noise = jnp.clip(jax.random.normal(noise_key, (SEG, NCH, TP * TQ + 3), jnp.float32), -4.0, 4.0)
    taps = jax.random.uniform(taps_key, (3, NCH), jnp.float32, -0.9, 0.9)
    signal = noise[:, :, 3:] + taps[0][None, :, None] * noise[:, :, 2:-1] + taps[1][None, :, None] * noise[:, :, 1:-2] + taps[2][None, :, None] * noise[:, :, :-3]
    return signal.astype(jnp.bfloat16)


def draw_source_index(key, part):
    key = jax.random.fold_in(key, 23)
    inner_key, order_key = jax.random.split(key)
    inner = jax.random.permutation(inner_key, NCH - 2)[:NS - 2].astype(jnp.int32) + 1
    picked = jnp.concatenate([jnp.array([0, NCH - 1], dtype=jnp.int32), inner])
    order = jax.random.permutation(order_key, NS)
    return picked[order].astype(jnp.int32)


def draw_band_edges(key, part):
    key = jax.random.fold_in(key, 37)
    spare = NF - NB * BAND_MIN
    cuts = jnp.sort(jax.random.randint(key, (NB - 1,), 0, spare + 1, dtype=jnp.int32))
    bounds = jnp.concatenate([jnp.zeros((1,), jnp.int32), cuts, jnp.full((1,), spare, jnp.int32)])
    widths = bounds[1:] - bounds[:-1] + BAND_MIN
    return jnp.concatenate([jnp.zeros((1,), jnp.int32), jnp.cumsum(widths).astype(jnp.int32)])


def setup_inputs(seed: int = 0) -> dict:
    key_of = jax.random.split(jax.random.key(seed), 4)
    return {
        "records": draw_records(jax.random.fold_in(key_of[3], 71), 0),
        "source_index": draw_source_index(jax.random.fold_in(key_of[3], 71), 0),
        "band_edges": draw_band_edges(jax.random.fold_in(key_of[3], 71), 0),
    }


epsilon = 1e-06
clip_factor = 2.0
peak_value = lax.Precision.HIGHEST

def whiten(spec_re, spec_im, band_edges):
    bin_index = jnp.arange(spec_re.shape[-1], dtype=jnp.int32)
    member = ((bin_index[None, :] >= band_edges[:-1, None]) & (bin_index[None, :] < band_edges[1:, None])).astype(jnp.float32)
    power = spec_re * spec_re + spec_im * spec_im
    band_total = jnp.dot(power, member.T, precision=peak_value)
    band_mean = band_total / lax.optimization_barrier(jnp.sum(member, axis=1))
    per_bin = jnp.dot(band_mean, member, precision=peak_value)
    scaling = lax.rsqrt(per_bin + epsilon)
    return (spec_re * scaling, spec_im * scaling)

def reference(records, source_index, band_edges):
    signal = records.astype(jnp.float32)
    amplitude = jnp.sqrt(lax.optimization_barrier(jnp.mean(signal * signal, axis=-1, keepdims=True)) + epsilon)
    clipped = jnp.clip(signal, -clip_factor * amplitude, clip_factor * amplitude)
    spectrum = jnp.fft.rfft(clipped, axis=-1)[:, :, F_LOW:F_LOW + NF]
    white_re, white_im = whiten(jnp.real(spectrum).astype(jnp.float32), jnp.imag(spectrum).astype(jnp.float32), band_edges)
    source_re = white_re[:, source_index, :]
    source_im = white_im[:, source_index, :]
    block_size = 16
    block_count = NF // block_size

    def arrange(values):
        shaped = values.reshape(values.shape[0], values.shape[1], block_count, block_size)
        return shaped.transpose(2, 3, 0, 1)

    def one_block(operands):
        receiver_real, receiver_imaginary, selected_real, selected_imaginary = operands
        real_component = jnp.einsum('ynm,ynb->ymb', selected_real, receiver_real, precision=peak_value) + jnp.einsum('ynm,ynb->ymb', selected_imaginary, receiver_imaginary, precision=peak_value)
        imaginary_component = jnp.einsum('ynm,ynb->ymb', selected_real, receiver_imaginary, precision=peak_value) - jnp.einsum('ynm,ynb->ymb', selected_imaginary, receiver_real, precision=peak_value)
        return (jnp.stack([real_component, imaginary_component], axis=1) / SEG).astype(jnp.bfloat16)
    blocks = lax.map(one_block, (arrange(white_re), arrange(white_im), arrange(source_re), arrange(source_im)))
    return blocks.reshape(NF, 2, NS, NCH)
```

```python
import functools

import jax
import jax.numpy as jnp
import numpy as np
from jax import lax
from jax.experimental import pallas as pl
from jax.experimental.pallas import tpu as pltpu
from jax.sharding import PartitionSpec as P

SEG = 8
NSAMP = 7680
F_LOW = 7
NF = 1536
NB = 32
NS = 64
NDEV = 64
NBIN = 24
CH = 10
HOP = NSAMP // NBIN
HPAD = 384
GROUPS = 3
ROWS = 32
RECV = NDEV * CH

EPS = 1e-06
CLIP = 2.0
F32 = jnp.float32
BF16 = jnp.bfloat16
NT = (((1,), (1,)), ((), ()))
VMEM_LIMIT = 48 * 1024 * 1024


def split_np(values):
    hi = values.astype(jnp.bfloat16)
    lo = (values - hi.astype(np.float64)).astype(jnp.bfloat16)
    return hi, lo


@functools.lru_cache(maxsize=None)
def tables():
    m = np.arange(HPAD)
    inside = (m < HOP).astype(np.float64)
    s = np.arange(NBIN) + F_LOW
    angle = 2.0 * np.pi * ((s[:, None] * m[None, :]) % NSAMP) / NSAMP
    twiddle = np.stack([np.cos(angle) * inside, -np.sin(angle) * inside], axis=1)
    d = np.arange(NDEV)
    angle = 2.0 * np.pi * ((m[:, None] * d[None, :]) % HOP) / HOP
    cos, sin = np.cos(angle) * inside[:, None], np.sin(angle) * inside[:, None]
    w = np.concatenate(
        [np.concatenate([cos, -sin], axis=1), np.concatenate([sin, cos], axis=1)], axis=0
    )
    w_hi, w_lo = split_np(w)
    return (
        twiddle.reshape(2 * NBIN, HPAD).astype(np.float32),
        np.concatenate([w_hi, w_lo], axis=1),
    )


def split(x):
    hi = x.astype(BF16)
    lo = (x - hi.astype(F32)).astype(BF16)
    return hi, lo


def real_dft8(x):
    r = np.float32(np.sqrt(0.5))
    e0, e1, e2, e3 = x[0] + x[4], x[1] + x[5], x[2] + x[6], x[3] + x[7]
    f0, f1, f2, f3 = x[0] - x[4], x[1] - x[5], x[2] - x[6], x[3] - x[7]
    g0, g1 = e0 + e2, e1 + e3
    p, q = (f1 - f3) * r, (f1 + f3) * r
    return [
        (g0 + g1, None),
        (f0 + p, -(f2 + q)),
        (e0 - e2, e3 - e1),
        (f0 - p, f2 - q),
        (g0 - g1, None),
    ]


def real_dft24(x):
    h = np.float32(np.sqrt(3.0) / 2.0)
    parts = [real_dft8([x[(8 * a + 3 * b) % 24] for b in range(8)]) for a in range(3)]
    out = [None] * 24

    def put(ka, kb, re, im):
        k = (16 * ka + 9 * kb) % 24
        out[k] = (re, im)
        if (24 - k) % 24 != k:
            out[24 - k] = (re, None if im is None else -im)

    for kb in range(5):
        (r0, i0), (r1, i1), (r2, i2) = (parts[a][kb] for a in range(3))
        sr, dr = r1 + r2, (r1 - r2) * h
        cr = r0 - 0.5 * sr
        if i0 is None:
            put(0, kb, r0 + sr, None)
            put(1, kb, cr, -dr)
        else:
            si, di = i1 + i2, (i1 - i2) * h
            ci = i0 - 0.5 * si
            put(0, kb, r0 + sr, i0 + si)
            put(1, kb, cr + di, ci - dr)
            put(2, kb, cr - di, ci + dr)
    return out


def spectra_kernel(rec_ref, lo_ref, hi_ref, tw_ref, w_ref, out_ref, x_ref, a_ref, z_ref, p_ref):
    lane = lax.broadcasted_iota(jnp.int32, (SEG, 128), 1)
    low_half = lane < 64

    for seg in range(SEG):
        for n in range(NSAMP // 128):
            x_ref[pl.ds(n * 128 + seg * 16, CH), :] = rec_ref[seg, :, pl.ds(n * 128, 128)].astype(F32)

    def channel(i, carry):
        def tile(n):
            return x_ref[pl.ds(n * 128 + i, SEG, stride=16), :]

        total = [None] * 4
        for n in range(NSAMP // 128):
            v = tile(n)
            total[n % 4] = v * v if total[n % 4] is None else total[n % 4] + v * v
        power = jnp.sum((total[0] + total[1]) + (total[2] + total[3]), axis=1, keepdims=True)
        bound = jnp.broadcast_to(CLIP * jnp.sqrt(power * (1.0 / NSAMP) + EPS), (SEG, 128))

        def clipped(n):
            return jnp.minimum(jnp.maximum(tile(n), -bound), bound)

        for q in range(3):
            x = []
            for a in range(NBIN):
                first = (a // 2) * 5
                if a % 2 == 0:
                    x.append(clipped(first + q))
                else:
                    left = pltpu.roll(clipped(first + 2 + q), 64, 1)
                    if q < 2:
                        right = pltpu.roll(clipped(first + 3 + q), 64, 1)
                        left = jnp.where(low_half, left, right)
                    x.append(left)
            y = real_dft24(x)
            for pair in range(NBIN // 2):
                res, ims = [], []
                for s in (2 * pair, 2 * pair + 1):
                    re, im = y[(s + F_LOW) % 24]
                    c = tw_ref[pl.ds(2 * s, 1), pl.ds(q * 128, 128)]
                    e = tw_ref[pl.ds(2 * s + 1, 1), pl.ds(q * 128, 128)]
                    if im is None:
                        res.append(re * c)
                        ims.append(re * e)
                    else:
                        res.append(re * c - im * e)
                        ims.append(re * e + im * c)
                for part, values in enumerate((res, ims)):
                    hi, lo = split(jnp.concatenate(values, axis=0))
                    a_ref[0, pl.ds(pair * 16, 16), pl.ds(part * HPAD + q * 128, 128)] = hi
                    a_ref[1, pl.ds(pair * 16, 16), pl.ds(part * HPAD + q * 128, 128)] = lo
        both = jnp.dot(a_ref[0], w_ref[...], preferred_element_type=F32)
        z = both[:, :128] + both[:, 128:]
        z = z + jnp.dot(a_ref[1], w_ref[:, :128], preferred_element_type=F32)
        row = pl.multiple_of(i * NBIN * SEG, NBIN * SEG)
        z_ref[pl.ds(row, NBIN * SEG), :] = z
        top = pl.multiple_of(i * SEG, SEG)
        for s in range(NBIN):
            v = z[s * SEG : (s + 1) * SEG]
            p_ref[pl.ds(top, SEG), pl.ds(s * 128, 128)] = v * v
        return carry

    lax.fori_loop(0, CH, channel, 0)

    shape = (NB, NBIN * 128)
    at = lax.broadcasted_iota(jnp.int32, shape, 1)
    bin_index = (at % 64) * NBIN + at // 128
    low, high = lo_ref[...], hi_ref[...]
    member = ((bin_index >= low) & (bin_index < high)).astype(F32).astype(BF16)
    p_hi, p_lo = split(p_ref[...])
    band = lax.dot_general(p_hi, member, NT, preferred_element_type=F32)
    band = band + lax.dot_general(p_lo, member, NT, preferred_element_type=F32)
    widths = jnp.sum(member.astype(F32), axis=1, keepdims=True) * 0.5
    eye = lax.broadcasted_iota(jnp.int32, (NB, NB), 0) == lax.broadcasted_iota(jnp.int32, (NB, NB), 1)
    widths = jnp.sum(jnp.where(eye, widths, 0.0), axis=0, keepdims=True)
    scale = lax.rsqrt(band / widths + EPS)
    s_hi = scale.astype(BF16)
    rest = scale - s_hi.astype(F32)
    s_mid, s_lo = split(rest)
    per_bin = jnp.dot(s_hi, member, preferred_element_type=F32)
    per_bin = per_bin + jnp.dot(s_mid, member, preferred_element_type=F32)
    per_bin = per_bin + jnp.dot(s_lo, member, preferred_element_type=F32)
    p_ref[...] = per_bin

    half64 = lax.broadcasted_iota(jnp.int32, (64, 128), 1) < 64

    def pair_of_channels(j, carry):
        for t in range(GROUPS):
            blocks = []
            for k in range(2):
                i = 2 * j + k
                z = z_ref[pl.ds(pl.multiple_of(i * NBIN * SEG, NBIN * SEG) + t * 64, 64), :]
                factor = jnp.concatenate(
                    [
                        p_ref[pl.ds(pl.multiple_of(i * SEG, SEG), SEG), pl.ds((t * 8 + u) * 128, 128)]
                        for u in range(8)
                    ],
                    axis=0,
                )
                blocks.append(z * factor)
            first, second = blocks
            upper = jnp.where(half64, first, pltpu.roll(second, 64, 1))
            lower = jnp.where(half64, pltpu.roll(first, 64, 1), second)
            turned = jnp.concatenate([upper, lower], axis=0).T
            out_ref[pl.ds(t * CH + 2 * j, NDEV, stride=ROWS), :] = turned[:64]
            out_ref[pl.ds(t * CH + 2 * j + 1, NDEV, stride=ROWS), :] = turned[64:]
        return carry

    lax.fori_loop(0, CH // 2, pair_of_channels, 0)
    for r in range(GROUPS * CH, ROWS):
        out_ref[pl.ds(r, NDEV, stride=ROWS), :] = jnp.zeros((NDEV, 128), F32)


def vmem():
    return pl.BlockSpec(memory_space=pltpu.VMEM)


def smem():
    return pl.BlockSpec(memory_space=pltpu.SMEM)


def spectra(records, band_edges):
    twiddle, w = tables()
    return pl.pallas_call(
        spectra_kernel,
        out_shape=jax.ShapeDtypeStruct((NDEV * ROWS, 128), F32),
        in_specs=[vmem()] * 5,
        out_specs=vmem(),
        scratch_shapes=[
            pltpu.VMEM((NSAMP, 128), F32),
            pltpu.VMEM((2, NBIN * SEG, 2 * HPAD), BF16),
            pltpu.VMEM((CH * NBIN * SEG, 128), F32),
            pltpu.VMEM((CH * SEG, NBIN * 128), F32),
        ],
        compiler_params=pltpu.CompilerParams(vmem_limit_bytes=VMEM_LIMIT),
        name="spectra",
    )(records, band_edges[:-1, None], band_edges[1:, None], jnp.asarray(twiddle), jnp.asarray(w))


def pick_kernel(local_ref, recv_ref, out_ref):
    def one(k, carry):
        local = local_ref[k]
        here = (local >= 0) & (local < RECV)
        place = jnp.clip(local, 0, RECV - 1)
        row = (place // CH) * ROWS + place % CH
        for t in range(GROUPS):
            v = recv_ref[pl.ds(row + t * CH, 1), :]
            out_ref[pl.ds(t * NS + k, 1), :] = jnp.where(here, v, 0.0)
        return carry

    lax.fori_loop(0, NS, one, 0)


def pick(local, received):
    return pl.pallas_call(
        pick_kernel,
        out_shape=jax.ShapeDtypeStruct((GROUPS * NS, 128), F32),
        in_specs=[smem(), vmem()],
        out_specs=vmem(),
        name="pick",
    )(local, received)


def pack_kernel(recv_ref, out_ref, dense_ref):
    for t in range(GROUPS):
        for i in range(CH):
            dense_ref[pl.ds(i, NDEV, stride=CH), :] = recv_ref[pl.ds(t * CH + i, NDEV, stride=ROWS), :]
        hi, lo = split(dense_ref[...])
        out_ref[t, :, pl.ds(0, 128)] = hi
        out_ref[t, :, pl.ds(128, 128)] = lo


def pack(received):
    return pl.pallas_call(
        pack_kernel,
        out_shape=jax.ShapeDtypeStruct((GROUPS, RECV, 256), BF16),
        in_specs=[vmem()],
        out_specs=vmem(),
        scratch_shapes=[pltpu.VMEM((RECV, 128), F32)],
        cost_estimate=pl.CostEstimate(flops=2000000, bytes_accessed=4000000, transcendentals=0),
        compiler_params=pltpu.CompilerParams(vmem_limit_bytes=VMEM_LIMIT),
        name="pack",
    )(received)


def correlate_kernel(src_ref, recv_ref, out_ref, left_ref, small_ref):
    s = src_ref[0]
    for b in range(1, src_ref.shape[0]):
        s = s + src_ref[b]
    s = s * (1.0 / SEG)
    lane = lax.broadcasted_iota(jnp.int32, (NS, 128), 1)
    turned = pltpu.roll(s, 64, 1)
    turned = jnp.where(lane < 64, -turned, turned)
    both = jnp.concatenate([s, turned], axis=0)
    hi, lo = split(both)
    which = lax.broadcasted_iota(jnp.int32, (2 * NS, 128), 1) // SEG % 8
    none = jnp.zeros_like(hi)
    for u in range(8):
        rows = pl.ds(u * 2 * NS, 2 * NS)
        chosen = jnp.where(which == u, hi, none)
        left_ref[rows, pl.ds(0, 128)] = chosen
        left_ref[rows, pl.ds(128, 128)] = chosen
        small_ref[rows, :] = jnp.where(which == u, lo, none)
    right = recv_ref[0]
    result = lax.dot_general(left_ref[...], right, NT, preferred_element_type=F32)
    result = result + lax.dot_general(small_ref[...], right[:, :128], NT, preferred_element_type=F32)
    out_ref[...] = result.astype(BF16).reshape(out_ref.shape)


def correlate(sources, packed):
    blocks = sources.shape[0]
    return pl.pallas_call(
        correlate_kernel,
        grid=(GROUPS,),
        out_shape=jax.ShapeDtypeStruct((NBIN, 2, NS, RECV), BF16),
        in_specs=[
            pl.BlockSpec((blocks, NS, 128), lambda t: (0, t, 0)),
            pl.BlockSpec((1, RECV, 256), lambda t: (t, 0, 0)),
        ],
        out_specs=pl.BlockSpec((8, 2, NS, RECV), lambda t: (t, 0, 0, 0)),
        scratch_shapes=[
            pltpu.VMEM((16 * NS, 256), BF16),
            pltpu.VMEM((16 * NS, 128), BF16),
        ],
        compiler_params=pltpu.CompilerParams(vmem_limit_bytes=VMEM_LIMIT),
        name="correlate",
    )(sources, packed)


def shards(records, source_index, band_edges):
    local = source_index - lax.axis_index("rblk") * RECV
    sent = spectra(records, band_edges)
    received = lax.all_to_all(sent, "chan", split_axis=0, concat_axis=0, tiled=True)
    picked = pick(local, received)
    sources = lax.all_gather(picked, "rblk", axis=0, tiled=False)
    packed = pack(received)
    return correlate(sources, packed)


def solution(mesh):
    return jax.shard_map(
        shards,
        mesh=mesh,
        in_specs=(P(None, ("rblk", "chan"), None), P(), P()),
        out_specs=P("chan", None, None, "rblk"),
        check_vma=False,
    )
```

```python
import functools

import jax
import jax.numpy as jnp
import numpy as np
from jax import lax
from jax.experimental import pallas as pl
from jax.experimental.pallas import tpu as pltpu
from jax.sharding import PartitionSpec as P

SEG = 8
NSAMP = 7680
F_LOW = 7
NF = 1536
NB = 32
NS = 64
NDEV = 64
NBIN = 24
CH = 10
HOP = NSAMP // NBIN
HPAD = 384
GROUPS = 3
ROWS = GROUPS * CH
ROOM = 20
RECV = NDEV * CH

EPS = 1e-06
CLIP = 2.0
F32 = jnp.float32
BF16 = jnp.bfloat16
NT = (((1,), (1,)), ((), ()))
VMEM_LIMIT = 40 * 1024 * 1024
FULL_VMEM = 60 * 1024 * 1024


def split_np(values):
    hi = values.astype(jnp.bfloat16)
    lo = (values - hi.astype(np.float64)).astype(jnp.bfloat16)
    return hi, lo


@functools.lru_cache(maxsize=None)
def tables():
    m = np.arange(HPAD)
    inside = (m < HOP).astype(np.float64)
    s = np.arange(NBIN) + F_LOW
    angle = 2.0 * np.pi * ((s[:, None] * m[None, :]) % NSAMP) / NSAMP
    twiddle = np.stack([np.cos(angle) * inside, -np.sin(angle) * inside], axis=1)
    d = np.arange(NDEV)
    angle = 2.0 * np.pi * ((m[:, None] * d[None, :]) % HOP) / HOP
    cos, sin = np.cos(angle) * inside[:, None], np.sin(angle) * inside[:, None]
    w = np.stack([np.concatenate([cos, -sin], axis=1), np.concatenate([sin, cos], axis=1)])
    w = w.reshape(2, 3, 128, 2 * NDEV).transpose(1, 0, 2, 3).reshape(2 * HPAD, 2 * NDEV)
    w_hi, w_lo = split_np(w)
    return (
        twiddle.reshape(2 * NBIN, HPAD).astype(np.float32),
        np.concatenate([w_hi, w_lo], axis=1),
    )


def split(x):
    hi = x.astype(BF16)
    lo = (x - hi.astype(F32)).astype(BF16)
    return hi, lo


def real_dft8(x):
    r = np.float32(np.sqrt(0.5))
    e0, e1, e2, e3 = x[0] + x[4], x[1] + x[5], x[2] + x[6], x[3] + x[7]
    f0, f1, f2, f3 = x[0] - x[4], x[1] - x[5], x[2] - x[6], x[3] - x[7]
    g0, g1 = e0 + e2, e1 + e3
    p, q = (f1 - f3) * r, (f1 + f3) * r
    return [
        (g0 + g1, None),
        (f0 + p, -(f2 + q)),
        (e0 - e2, e3 - e1),
        (f0 - p, f2 - q),
        (g0 - g1, None),
    ]


def real_dft24(x):
    h = np.float32(np.sqrt(3.0) / 2.0)
    parts = [real_dft8([x[(8 * a + 3 * b) % 24] for b in range(8)]) for a in range(3)]
    out = [None] * 24

    def put(ka, kb, re, im):
        k = (16 * ka + 9 * kb) % 24
        out[k] = (re, im)
        if (24 - k) % 24 != k:
            out[24 - k] = (re, None if im is None else -im)

    for kb in range(5):
        (r0, i0), (r1, i1), (r2, i2) = (parts[a][kb] for a in range(3))
        sr, dr = r1 + r2, (r1 - r2) * h
        cr = r0 - 0.5 * sr
        if i0 is None:
            put(0, kb, r0 + sr, None)
            put(1, kb, cr, -dr)
        else:
            si, di = i1 + i2, (i1 - i2) * h
            ci = i0 - 0.5 * si
            put(0, kb, r0 + sr, i0 + si)
            put(1, kb, cr + di, ci - dr)
            put(2, kb, cr - di, ci + dr)
    return out


def spectra_kernel(
    rec_hbm, edge_hbm, tw_hbm, w_hbm, out_ref,
    rec_ref, even_ref, odd_ref, z_ref, p_ref, m_ref, tw_ref, w_ref, edge_ref, rec_sems, sems,
):
    def fetch(i):
        return pltpu.make_async_copy(rec_hbm.at[i], rec_ref.at[i], rec_sems.at[i])

    small = [(edge_hbm, edge_ref), (tw_hbm, tw_ref), (w_hbm, w_ref)]
    copies = [pltpu.make_async_copy(a, b, sems.at[k]) for k, (a, b) in enumerate(small)]
    copies[0].start()
    fetch(0).start()
    copies[1].start()
    copies[2].start()
    for i in range(1, CH):
        fetch(i).start()

    copies[0].wait()
    shape = (NB, 128)
    row = lax.broadcasted_iota(jnp.int32, shape, 0)
    low, high = jnp.zeros(shape, jnp.int32), jnp.zeros(shape, jnp.int32)
    for k in range(NB):
        low = jnp.where(row == k, edge_ref[k], low)
        high = jnp.where(row == k, edge_ref[k + 1], high)
    widths = (high - low).astype(F32)
    eye = row == lax.broadcasted_iota(jnp.int32, shape, 1)
    widths = jnp.sum(jnp.where(eye, widths, 0.0), axis=0, keepdims=True)[:, :NB]
    start = (lax.broadcasted_iota(jnp.int32, shape, 1) & (NDEV - 1)) * NBIN
    for s in range(NBIN):
        inside = (start + s >= low) & (start + s < high)
        m_ref[:, pl.ds(s * 128, 128)] = jnp.where(inside, 1.0, 0.0).astype(BF16)
    copies[1].wait()
    copies[2].wait()

    lane = lax.broadcasted_iota(jnp.int32, (SEG, 128), 1)
    low_half = lane < 64

    def transform(i, a_ref):
        def tile(n):
            return rec_ref[i, :, pl.ds(n * 128, 128)].astype(F32)

        total = [None] * 4
        for n in range(NSAMP // 128):
            v = tile(n)
            total[n % 4] = v * v if total[n % 4] is None else total[n % 4] + v * v
        power = jnp.sum((total[0] + total[1]) + (total[2] + total[3]), axis=1, keepdims=True)
        bound = jnp.broadcast_to(CLIP * jnp.sqrt(power * (1.0 / NSAMP) + EPS), (SEG, 128))

        def clip(v):
            return jnp.minimum(jnp.maximum(v, -bound), bound)

        for q in range(3):
            x = []
            for a in range(NBIN):
                n = (a // 2) * 5 + q
                if a % 2 == 0:
                    x.append(clip(tile(n)))
                else:
                    left = tile(n + 2)
                    right = tile(n + 3) if q < 2 else left
                    x.append(clip(pltpu.roll(jnp.where(low_half, right, left), 64, 1)))
            y = real_dft24(x)
            for pair in range(NBIN // 2):
                res, ims = [], []
                for s in (2 * pair, 2 * pair + 1):
                    re, im = y[(s + F_LOW) % 24]
                    c = tw_ref[pl.ds(2 * s, 1), pl.ds(q * 128, 128)]
                    e = tw_ref[pl.ds(2 * s + 1, 1), pl.ds(q * 128, 128)]
                    if im is None:
                        res.append(re * c)
                        ims.append(re * e)
                    else:
                        res.append(re * c - im * e)
                        ims.append(re * e + im * c)
                for part, values in enumerate((res, ims)):
                    hi, lo = split(jnp.concatenate(values, axis=0))
                    a_ref[q, 0, pl.ds(pair * 16, 16), pl.ds(part * 128, 128)] = hi
                    a_ref[q, 1, pl.ds(pair * 16, 16), pl.ds(part * 128, 128)] = lo

    def multiply(place, a_ref):
        z = None
        for q in range(3):
            depth = pl.ds(q * 256, 256)
            both = jnp.dot(a_ref[q, 0], w_ref[depth, :], preferred_element_type=F32)
            rest = jnp.dot(a_ref[q, 1], w_ref[depth, pl.ds(0, 128)], preferred_element_type=F32)
            term = (both[:, :128] + both[:, 128:]) + rest
            z = term if z is None else z + term
        z_ref[pl.ds(pl.multiple_of(place * NBIN * SEG, NBIN * SEG), NBIN * SEG), :] = z
        for s in range(NBIN):
            v = z[s * SEG : (s + 1) * SEG]
            p_ref[pl.ds(pl.multiple_of(place * SEG, SEG), SEG), pl.ds(s * 128, 128)] = v * v

    def two_channels(j, carry):
        fetch(2 * j).wait()
        fetch(2 * j + 1).wait()
        multiply(2 * j, odd_ref)
        transform(2 * j, even_ref)
        multiply(2 * j + 1, even_ref)
        transform(2 * j + 1, odd_ref)
        return carry

    lax.fori_loop(0, CH // 2, two_channels, 0)
    multiply(CH, odd_ref)

    member = m_ref[...]
    rows = CH * SEG
    power = jnp.concatenate(split(p_ref[pl.ds(SEG, rows), :]), axis=0)
    band = lax.dot_general(power, member, NT, preferred_element_type=F32)
    band = band[:rows] + band[rows:]
    scale = lax.rsqrt(band / widths + EPS)
    s_hi = scale.astype(BF16)
    rest = scale - s_hi.astype(F32)
    s_mid, s_lo = split(rest)
    scales = jnp.concatenate([s_hi, s_mid, s_lo], axis=1)
    copied = jnp.concatenate([member] * 3, axis=0)
    per_bin = jnp.dot(scales, copied, preferred_element_type=F32)
    p_ref[pl.ds(SEG, CH * SEG), :] = per_bin

    half64 = lax.broadcasted_iota(jnp.int32, (64, 128), 1) < 64
    where = [(t, i) for i in range(CH) for t in range(GROUPS)]

    def whitened(t, i):
        z = z_ref[pl.ds((i + 1) * NBIN * SEG + t * 64, 64), :]
        factor = [p_ref[pl.ds((i + 1) * SEG, SEG), pl.ds((t * 8 + u) * 128, 128)] for u in range(8)]
        return z * jnp.concatenate(factor, axis=0)

    for k in range(0, len(where), 2):
        first, second = whitened(*where[k]), whitened(*where[k + 1])
        upper = jnp.where(half64, first, pltpu.roll(second, 64, 1))
        lower = jnp.where(half64, pltpu.roll(first, 64, 1), second)
        halves = [h[u * SEG : (u + 1) * SEG] for u in range(8) for h in (upper, lower)]
        turned = jnp.concatenate(halves, axis=0).T
        for part in range(2):
            t, i = where[k + part]
            out_ref[pl.ds(t * CH + i, NDEV, stride=ROWS), :] = turned[part * 64 : part * 64 + 64]


def vmem():
    return pl.BlockSpec(memory_space=pltpu.VMEM)


def smem():
    return pl.BlockSpec(memory_space=pltpu.SMEM)


def spectra(records, band_edges):
    twiddle, w = tables()
    return pl.pallas_call(
        spectra_kernel,
        out_shape=jax.ShapeDtypeStruct((NDEV * ROWS, 128), F32),
        in_specs=[pl.BlockSpec(memory_space=pltpu.HBM)] * 4,
        out_specs=vmem(),
        scratch_shapes=[
            pltpu.VMEM((CH, SEG, NSAMP), BF16),
            pltpu.VMEM((3, 2, NBIN * SEG, 256), BF16),
            pltpu.VMEM((3, 2, NBIN * SEG, 256), BF16),
            pltpu.VMEM(((CH + 1) * NBIN * SEG, 128), F32),
            pltpu.VMEM(((CH + 1) * SEG, NBIN * 128), F32),
            pltpu.VMEM((NB, NBIN * 128), BF16),
            pltpu.VMEM(twiddle.shape, F32),
            pltpu.VMEM(w.shape, BF16),
            pltpu.SMEM((NB + 1,), jnp.int32),
            pltpu.SemaphoreType.DMA((CH,)),
            pltpu.SemaphoreType.DMA((3,)),
        ],
        compiler_params=pltpu.CompilerParams(vmem_limit_bytes=FULL_VMEM),
        name="spectra",
    )(records, band_edges, jnp.asarray(twiddle), jnp.asarray(w))


def pick_kernel(copies, rows, ordered, place_ref, recv_ref, out_ref, held_ref):
    held_ref[...] = jnp.zeros_like(held_ref)

    def one(n, carry):
        to = place_ref[0, n] if ordered else n
        held_ref[pl.ds(to * GROUPS, GROUPS), :] = recv_ref[pl.ds(place_ref[1, n], GROUPS, stride=CH), :]
        return carry

    lax.fori_loop(0, place_ref[2, 0], one, 0)
    for k in range(copies):
        out_ref[pl.ds(k * rows, rows), :] = held_ref[...]


def pick(places, received, copies, room, ordered):
    rows = room * GROUPS
    return pl.pallas_call(
        functools.partial(pick_kernel, copies, rows, ordered),
        out_shape=jax.ShapeDtypeStruct((copies * rows, 128), F32),
        in_specs=[smem(), vmem()],
        out_specs=vmem(),
        scratch_shapes=[pltpu.VMEM((rows, 128), F32)],
        compiler_params=pltpu.CompilerParams(vmem_limit_bytes=VMEM_LIMIT),
        name="pick",
    )(places, received)


def correlate_kernel(at_ref, src_ref, recv_ref, out_hbm, left_ref, right_ref, dense_ref, s_ref, out_ref, sems):
    for k in range(NS):
        s_ref[pl.ds(k * GROUPS, GROUPS), :] = src_ref[pl.ds(at_ref[k], GROUPS), :]
    lower = lax.broadcasted_iota(jnp.int32, (RECV, 128), 1) < 64
    lane = lax.broadcasted_iota(jnp.int32, (2 * NS, 128), 1)
    imag = lane[:NS] & SEG != 0
    which = lane // (2 * SEG)
    copies = []
    for t in range(GROUPS):
        for i in range(CH):
            dense_ref[t, pl.ds(i, NDEV, stride=CH), :] = recv_ref[pl.ds(t * CH + i, NDEV, stride=ROWS), :]

        hi, lo = split(dense_ref[t])
        turned = pltpu.roll(lo.astype(F32), 64, 1).astype(BF16)
        right_ref[t, 0] = jnp.where(lower, hi, turned)
        right_ref[t, 1] = jnp.where(lower, turned, hi)
        right_ref[t, 2] = hi

        s = s_ref[pl.ds(t, NS, stride=GROUPS), :] * (1.0 / SEG)
        crossed = jnp.where(imag, pltpu.roll(s, SEG, 1), -pltpu.roll(s, 128 - SEG, 1))
        hi, lo = split(jnp.concatenate([s, crossed], axis=0))
        hi, lo = hi.astype(F32), lo.astype(F32)
        hi_turned = pltpu.roll(hi, 64, 1)
        for h in range(2):
            part = 2 * t + h
            both = jnp.where((lane < 64) == (h == 0), hi, hi_turned)
            for v in range(4):
                rows = pl.ds(v * 2 * NS, 2 * NS)
                left_ref[part, rows, pl.ds(0, 128)] = jnp.where(which % 4 == v, both, 0.0).astype(BF16)
                left_ref[part, rows, pl.ds(128, 128)] = jnp.where(which == 4 * h + v, lo, 0.0).astype(BF16)
            right = jnp.concatenate([right_ref[t, h], right_ref[t, 2]], axis=1)
            result = lax.dot_general(left_ref[part], right, NT, preferred_element_type=F32)
            bins = pl.ds(4 * part, 4)
            out_ref[bins] = result.astype(BF16).reshape(4, 2, NS, RECV)
            copies.append(pltpu.make_async_copy(out_ref.at[bins], out_hbm.at[bins], sems.at[part]))
            copies[-1].start()
    for copy in copies:
        copy.wait()


def correlate(at, sources, received):
    parts = 2 * GROUPS
    return pl.pallas_call(
        correlate_kernel,
        out_shape=jax.ShapeDtypeStruct((NBIN, 2, NS, RECV), BF16),
        in_specs=[smem(), vmem(), vmem()],
        out_specs=pl.BlockSpec(memory_space=pltpu.HBM),
        scratch_shapes=[
            pltpu.VMEM((parts, 8 * NS, 256), BF16),
            pltpu.VMEM((GROUPS, 3, RECV, 128), BF16),
            pltpu.VMEM((GROUPS, RECV, 128), F32),
            pltpu.VMEM((NS * GROUPS, 128), F32),
            pltpu.VMEM((NBIN, 2, NS, RECV), BF16),
            pltpu.SemaphoreType.DMA((parts,)),
        ],
        compiler_params=pltpu.CompilerParams(vmem_limit_bytes=VMEM_LIMIT),
        name="correlate",
    )(at, sources, received)


def plan(source_index, block):
    owner, local = source_index // RECV, source_index % RECV
    number = jnp.arange(NS, dtype=jnp.int32)
    same = owner[:, None] == owner[None, :]
    rank = jnp.sum(same & (number[None, :] < number[:, None]), axis=1, dtype=jnp.int32)
    crowded = jnp.any(rank >= ROOM)
    chosen = owner == block
    to = (chosen & (rank == number[:, None]))[None]
    row = local // CH * ROWS + local % CH
    columns = jnp.stack([number, row, jnp.ones_like(row)])[:, None, :]
    places = jnp.sum(jnp.where(to, columns, 0), axis=2)
    total = jnp.sum(chosen, dtype=jnp.int32)
    places = jnp.concatenate([places[:2], jnp.broadcast_to(total, (1, NS))])
    at = GROUPS * jnp.where(crowded, number, owner * ROOM + rank)
    return places, at, crowded


def share(places, received, blocks):
    rows = pick(places, received, blocks, ROOM, False)
    flat = rows.reshape(blocks, 1, ROOM * GROUPS * 128)
    return lax.all_to_all(flat, "rblk", split_axis=0, concat_axis=0, tiled=True).reshape(rows.shape)


def share_all(places, received, blocks):
    rows = pick(places, received, 1, NS, True)
    total = jnp.sum(lax.all_gather(rows, "rblk", axis=0, tiled=False), axis=0)
    return jnp.pad(total, ((0, (blocks * ROOM - NS) * GROUPS), (0, 0)))


def shards(records, source_index, band_edges):
    blocks = lax.axis_size("rblk")
    places, at, crowded = plan(source_index, lax.axis_index("rblk"))
    sent = spectra(jnp.transpose(records, (1, 0, 2)), band_edges)
    flat = sent.reshape(NDEV, 1, ROWS * 128)
    received = lax.all_to_all(flat, "chan", split_axis=0, concat_axis=0, tiled=True).reshape(sent.shape)
    sources = lax.cond(
        crowded,
        functools.partial(share_all, blocks=blocks),
        functools.partial(share, blocks=blocks),
        places,
        received,
    )
    return correlate(at, sources, received)


def solution(mesh):
    return jax.shard_map(
        shards,
        mesh=mesh,
        in_specs=(P(None, ("rblk", "chan"), None), P(), P()),
        out_specs=P("chan", None, None, "rblk"),
        check_vma=False,
    )
```

```python
import functools

import jax
import jax.numpy as jnp
import numpy as np
from jax import lax
from jax.experimental import pallas as pl
from jax.experimental.pallas import tpu as pltpu
from jax.sharding import PartitionSpec as P

SEG = 8
NSAMP = 7680
F_LOW = 7
NF = 1536
NB = 32
NS = 64
NDEV = 64
NBIN = 24
CH = 10
HOP = NSAMP // NBIN
HPAD = 384
GROUPS = 3
ROWS = GROUPS * CH
ROOM = 16
RECV = NDEV * CH

EPS = 1e-06
CLIP = 2.0
F32 = jnp.float32
BF16 = jnp.bfloat16
NT = (((1,), (1,)), ((), ()))
VMEM_LIMIT = 40 * 1024 * 1024
FULL_VMEM = 60 * 1024 * 1024


def split_np(values):
    hi = values.astype(jnp.bfloat16)
    lo = (values - hi.astype(np.float64)).astype(jnp.bfloat16)
    return hi, lo


@functools.lru_cache(maxsize=None)
def tables():
    m = np.arange(HPAD)
    s = np.arange(NBIN) + F_LOW
    angle = 2.0 * np.pi * ((s[:, None] * m[None, :]) % NSAMP) / NSAMP
    twiddle = np.stack([np.cos(angle), -np.sin(angle)], axis=1)
    d = np.arange(NDEV)
    angle = 2.0 * np.pi * ((m[:HOP, None] * d[None, :]) % HOP) / HOP
    cos, sin = np.cos(angle), np.sin(angle)
    of_re, of_im = np.concatenate([cos, -sin], axis=1), np.concatenate([sin, cos], axis=1)
    cuts = [slice(0, 128), slice(128, 256), slice(256, HOP)]
    w_hi, w_lo = split_np(np.concatenate([part[cut] for cut in cuts for part in (of_re, of_im)]))
    both = np.concatenate([w_hi, w_lo], axis=1)
    last = np.concatenate([w_hi[512:], np.zeros_like(w_lo[512:])], axis=1)
    return twiddle.reshape(2 * NBIN, HPAD).astype(np.float32), np.concatenate([both, last])


def split(x):
    hi = x.astype(BF16)
    lo = (x - hi.astype(F32)).astype(BF16)
    return hi, lo


def real_dft8(x):
    r = np.float32(np.sqrt(0.5))
    e0, e1, e2, e3 = x[0] + x[4], x[1] + x[5], x[2] + x[6], x[3] + x[7]
    f0, f1, f2, f3 = x[0] - x[4], x[1] - x[5], x[2] - x[6], x[3] - x[7]
    g0, g1 = e0 + e2, e1 + e3
    p, q = (f1 - f3) * r, (f1 + f3) * r
    return [
        (g0 + g1, None),
        (f0 + p, -(f2 + q)),
        (e0 - e2, e3 - e1),
        (f0 - p, f2 - q),
        (g0 - g1, None),
    ]


def real_dft24(x):
    h = np.float32(np.sqrt(3.0) / 2.0)
    parts = [real_dft8([x[(8 * a + 3 * b) % 24] for b in range(8)]) for a in range(3)]
    out = [None] * 24

    def put(ka, kb, re, im):
        k = (16 * ka + 9 * kb) % 24
        out[k] = (re, im)
        if (24 - k) % 24 != k:
            out[24 - k] = (re, None if im is None else -im)

    for kb in range(5):
        (r0, i0), (r1, i1), (r2, i2) = (parts[a][kb] for a in range(3))
        sr, dr = r1 + r2, (r1 - r2) * h
        cr = r0 - 0.5 * sr
        if i0 is None:
            put(0, kb, r0 + sr, None)
            put(1, kb, cr, -dr)
        else:
            si, di = i1 + i2, (i1 - i2) * h
            ci = i0 - 0.5 * si
            put(0, kb, r0 + sr, i0 + si)
            put(1, kb, cr + di, ci - dr)
            put(2, kb, cr - di, ci + dr)
    return out


def spectra_kernel(
    rec_hbm, edge_hbm, tw_hbm, w_hbm, out_ref,
    rec_ref, even_ref, odd_ref, z_ref, p_ref, m_ref, tw_ref, w_ref, edge_ref, rec_sems, sems,
):
    def fetch(i):
        return pltpu.make_async_copy(rec_hbm.at[i], rec_ref.at[i], rec_sems.at[i])

    small = [(edge_hbm, edge_ref), (tw_hbm, tw_ref), (w_hbm, w_ref)]
    edge_copy, tw_copy, w_copy = [pltpu.make_async_copy(a, b, sems.at[k]) for k, (a, b) in enumerate(small)]
    edge_copy.start()
    fetch(0).start()
    tw_copy.start()
    fetch(1).start()
    w_copy.start()
    for i in range(2, CH):
        fetch(i).start()

    edge_copy.wait()
    shape = (NB, 128)
    row = lax.broadcasted_iota(jnp.int32, shape, 0)
    low, high = jnp.zeros(shape, jnp.int32), jnp.zeros(shape, jnp.int32)
    for k in range(NB):
        low = jnp.where(row == k, edge_ref[k], low)
        high = jnp.where(row == k, edge_ref[k + 1], high)
    widths = (high - low).astype(F32)
    eye = row == lax.broadcasted_iota(jnp.int32, shape, 1)
    widths = jnp.sum(jnp.where(eye, widths, 0.0), axis=0, keepdims=True)[:, :NB]
    start = (lax.broadcasted_iota(jnp.int32, shape, 1) & (NDEV - 1)) * NBIN
    for s in range(NBIN):
        inside = (start + s >= low) & (start + s < high)
        m_ref[:, pl.ds(s * 128, 128)] = jnp.where(inside, 1.0, 0.0).astype(BF16)
    tw_copy.wait()

    lane = lax.broadcasted_iota(jnp.int32, (SEG, 128), 1)
    low_half = lane < 64

    def transform(i, a_ref):
        def tile(n):
            return rec_ref[i, :, pl.ds(n * 128, 128)].astype(F32)

        total = [None] * 4
        for n in range(NSAMP // 128):
            v = tile(n)
            total[n % 4] = v * v if total[n % 4] is None else total[n % 4] + v * v
        power = jnp.sum((total[0] + total[1]) + (total[2] + total[3]), axis=1, keepdims=True)
        bound = jnp.broadcast_to(CLIP * jnp.sqrt(power * (1.0 / NSAMP) + EPS), (SEG, 128))

        def clip(v):
            return jnp.minimum(jnp.maximum(v, -bound), bound)

        for q in range(3):
            x = []
            for a in range(NBIN):
                n = (a // 2) * 5 + q
                if a % 2 == 0:
                    x.append(clip(tile(n)))
                else:
                    left = tile(n + 2)
                    right = tile(n + 3) if q < 2 else left
                    x.append(clip(pltpu.roll(jnp.where(low_half, right, left), 64, 1)))
            y = real_dft24(x)
            for pair in range(NBIN // 2):
                res, ims = [], []
                for s in (2 * pair, 2 * pair + 1):
                    re, im = y[(s + F_LOW) % 24]
                    c = tw_ref[pl.ds(2 * s, 1), pl.ds(q * 128, 128)]
                    e = tw_ref[pl.ds(2 * s + 1, 1), pl.ds(q * 128, 128)]
                    if im is None:
                        res.append(re * c)
                        ims.append(re * e)
                    else:
                        res.append(re * c - im * e)
                        ims.append(re * e + im * c)
                rows = pl.ds(pair * 16, 16)
                if q == 2:
                    values = [jnp.where(low_half, r, pltpu.roll(i, 64, 1)) for r, i in zip(res, ims)]
                    hi, lo = split(jnp.concatenate(values, axis=0))
                    a_ref[4, rows, pl.ds(0, 128)] = hi
                    a_ref[4, rows, pl.ds(128, 128)] = lo
                    continue
                for part, values in enumerate((res, ims)):
                    hi, lo = split(jnp.concatenate(values, axis=0))
                    a_ref[q, rows, pl.ds(part * 128, 128)] = hi
                    a_ref[2 + q, rows, pl.ds(part * 128, 128)] = lo

    def multiply(i, a_ref):
        both = jnp.dot(a_ref[0], w_ref[pl.ds(0, 256), :], preferred_element_type=F32)
        both = both + jnp.dot(a_ref[1], w_ref[pl.ds(256, 256), :], preferred_element_type=F32)
        both = both + jnp.dot(a_ref[4], w_ref[pl.ds(512, 256), :], preferred_element_type=F32)
        rest = jnp.dot(a_ref[2], w_ref[pl.ds(0, 256), pl.ds(0, 128)], preferred_element_type=F32)
        rest = rest + jnp.dot(a_ref[3], w_ref[pl.ds(256, 256), pl.ds(0, 128)], preferred_element_type=F32)
        z = (both[:, :128] + both[:, 128:]) + rest
        z_ref[pl.ds(i * NBIN * SEG, NBIN * SEG), :] = z
        for s in range(NBIN):
            v = z[s * SEG : (s + 1) * SEG]
            p_ref[pl.ds(i * SEG, SEG), pl.ds(s * 128, 128)] = v * v

    half64 = lax.broadcasted_iota(jnp.int32, (64, 128), 1) < 64

    def whiten():
        rows = CH * SEG
        member = m_ref[...]
        power = jnp.concatenate(split(p_ref[...]), axis=0)
        band = lax.dot_general(power, member, NT, preferred_element_type=F32)
        scale = lax.rsqrt((band[:rows] + band[rows:]) / widths + EPS)
        s_hi = scale.astype(BF16)
        s_mid, s_lo = split(scale - s_hi.astype(F32))
        scales = jnp.concatenate([s_hi, s_mid, s_lo], axis=1)
        copied = jnp.concatenate([member] * 3, axis=0)
        p_ref[...] = jnp.dot(scales, copied, preferred_element_type=F32)

    def whitened(t, i):
        z = z_ref[pl.ds(i * NBIN * SEG + t * 64, 64), :]
        factor = [p_ref[pl.ds(i * SEG, SEG), pl.ds((t * 8 + u) * 128, 128)] for u in range(8)]
        return z * jnp.concatenate(factor, axis=0)

    def place(*pair):
        first, second = (whitened(t, i) for t, i in pair)
        upper = jnp.where(half64, first, pltpu.roll(second, 64, 1))
        lower = jnp.where(half64, pltpu.roll(first, 64, 1), second)
        halves = [h[u * SEG : (u + 1) * SEG] for u in range(8) for h in (upper, lower)]
        turned = jnp.concatenate(halves, axis=0).T
        for part, (t, i) in enumerate(pair):
            out_ref[pl.ds(t * CH + i, NDEV, stride=ROWS), :] = turned[part * 64 : part * 64 + 64]

    a_refs = (even_ref, odd_ref)
    for i in range(CH):
        fetch(i).wait()
        if i:
            multiply(i - 1, a_refs[(i - 1) % 2])
        transform(i, a_refs[i % 2])
        if i == 0:
            w_copy.wait()
    multiply(CH - 1, a_refs[(CH - 1) % 2])
    whiten()
    for i in range(0, CH, 2):
        for t in range(GROUPS):
            place((t, i), (t, i + 1))


def vmem():
    return pl.BlockSpec(memory_space=pltpu.VMEM)


def smem():
    return pl.BlockSpec(memory_space=pltpu.SMEM)


def spectra(records, band_edges):
    twiddle, w = tables()
    return pl.pallas_call(
        spectra_kernel,
        out_shape=jax.ShapeDtypeStruct((NDEV * ROWS, 128), F32),
        in_specs=[pl.BlockSpec(memory_space=pltpu.HBM)] * 4,
        out_specs=vmem(),
        scratch_shapes=[
            pltpu.VMEM((CH, SEG, NSAMP), BF16),
            pltpu.VMEM((5, NBIN * SEG, 256), BF16),
            pltpu.VMEM((5, NBIN * SEG, 256), BF16),
            pltpu.VMEM((CH * NBIN * SEG, 128), F32),
            pltpu.VMEM((CH * SEG, NBIN * 128), F32),
            pltpu.VMEM((NB, NBIN * 128), BF16),
            pltpu.VMEM(twiddle.shape, F32),
            pltpu.VMEM(w.shape, BF16),
            pltpu.SMEM((NB + 1,), jnp.int32),
            pltpu.SemaphoreType.DMA((CH,)),
            pltpu.SemaphoreType.DMA((3,)),
        ],
        compiler_params=pltpu.CompilerParams(vmem_limit_bytes=FULL_VMEM),
        name="spectra",
    )(records, band_edges, jnp.asarray(twiddle), jnp.asarray(w))


def pick_kernel(copies, rows, ordered, place_ref, recv_ref, out_ref, held_ref):
    held_ref[...] = jnp.zeros_like(held_ref)

    def one(n, carry):
        to = place_ref[0, n] if ordered else n
        held_ref[pl.ds(to * GROUPS, GROUPS), :] = recv_ref[pl.ds(place_ref[1, n], GROUPS, stride=CH), :]
        return carry

    lax.fori_loop(0, place_ref[2, 0], one, 0)
    for k in range(copies):
        out_ref[pl.ds(k * rows, rows), :] = held_ref[...]


def pick(places, received, copies, room, ordered):
    rows = room * GROUPS
    return pl.pallas_call(
        functools.partial(pick_kernel, copies, rows, ordered),
        out_shape=jax.ShapeDtypeStruct((copies * rows, 128), F32),
        in_specs=[smem(), vmem()],
        out_specs=vmem(),
        scratch_shapes=[pltpu.VMEM((rows, 128), F32)],
        compiler_params=pltpu.CompilerParams(vmem_limit_bytes=VMEM_LIMIT),
        name="pick",
    )(places, received)


def correlate_kernel(
    at_hbm, src_ref, recv_ref, out_hbm, left_ref, right_ref, dense_ref, s_ref, out_ref, at_ref, at_sem, sems
):
    table = pltpu.make_async_copy(at_hbm, at_ref, at_sem)
    table.start()
    lower = lax.broadcasted_iota(jnp.int32, (RECV, 128), 1) < 64
    lane = lax.broadcasted_iota(jnp.int32, (2 * NS, 128), 1)
    imag = lane[:NS] & SEG != 0
    which = lane // (2 * SEG)
    copies = []
    for t in range(GROUPS):
        for i in range(CH):
            dense_ref[t, pl.ds(i, NDEV, stride=CH), :] = recv_ref[pl.ds(t * CH + i, NDEV, stride=ROWS), :]

        hi, lo = split(dense_ref[t])
        turned = pltpu.roll(lo.astype(F32), 64, 1).astype(BF16)
        right_ref[t, 0] = jnp.where(lower, hi, turned)
        right_ref[t, 1] = jnp.where(lower, turned, hi)
        right_ref[t, 2] = hi

        if t == 0:
            table.wait()
            for k in range(NS):
                s_ref[pl.ds(k * GROUPS, GROUPS), :] = src_ref[pl.ds(at_ref[k], GROUPS), :]
        s = s_ref[pl.ds(t, NS, stride=GROUPS), :] * (1.0 / SEG)
        crossed = jnp.where(imag, pltpu.roll(s, SEG, 1), -pltpu.roll(s, 128 - SEG, 1))
        hi, lo = split(jnp.concatenate([s, crossed], axis=0))
        hi, lo = hi.astype(F32), lo.astype(F32)
        hi_turned = pltpu.roll(hi, 64, 1)
        for h in range(2):
            part = 2 * t + h
            both = jnp.where((lane < 64) == (h == 0), hi, hi_turned)
            for v in range(4):
                rows = pl.ds(v * 2 * NS, 2 * NS)
                left_ref[part, rows, pl.ds(0, 128)] = jnp.where(which % 4 == v, both, 0.0).astype(BF16)
                left_ref[part, rows, pl.ds(128, 128)] = jnp.where(which == 4 * h + v, lo, 0.0).astype(BF16)
            right = jnp.concatenate([right_ref[t, h], right_ref[t, 2]], axis=1)
            for w in range(2):
                left = left_ref[part, pl.ds(w * 4 * NS, 4 * NS)]
                result = lax.dot_general(left, right, NT, preferred_element_type=F32)
                piece = 2 * part + w
                bins = pl.ds(2 * piece, 2)
                out_ref[bins] = result.astype(BF16).reshape(2, 2, NS, RECV)
                copies.append(pltpu.make_async_copy(out_ref.at[bins], out_hbm.at[bins], sems.at[piece]))
                copies[-1].start()
    for copy in copies:
        copy.wait()


def correlate(at, sources, received):
    parts = 2 * GROUPS
    return pl.pallas_call(
        correlate_kernel,
        out_shape=jax.ShapeDtypeStruct((NBIN, 2, NS, RECV), BF16),
        in_specs=[pl.BlockSpec(memory_space=pltpu.HBM), vmem(), vmem()],
        out_specs=pl.BlockSpec(memory_space=pltpu.HBM),
        scratch_shapes=[
            pltpu.VMEM((parts, 8 * NS, 256), BF16),
            pltpu.VMEM((GROUPS, 3, RECV, 128), BF16),
            pltpu.VMEM((GROUPS, RECV, 128), F32),
            pltpu.VMEM((NS * GROUPS, 128), F32),
            pltpu.VMEM((NBIN, 2, NS, RECV), BF16),
            pltpu.SMEM((NS,), jnp.int32),
            pltpu.SemaphoreType.DMA,
            pltpu.SemaphoreType.DMA((2 * parts,)),
        ],
        compiler_params=pltpu.CompilerParams(vmem_limit_bytes=VMEM_LIMIT),
        name="correlate",
    )(at, sources, received)


def plan(source_index, block):
    owner, local = source_index // RECV, source_index % RECV
    number = jnp.arange(NS, dtype=jnp.int32)
    same = owner[:, None] == owner[None, :]
    rank = jnp.sum(same & (number[None, :] < number[:, None]), axis=1, dtype=jnp.int32)
    crowded = jnp.any(rank >= ROOM)
    chosen = owner == block
    to = (chosen & (rank == number[:, None]))[None]
    row = local // CH * ROWS + local % CH
    columns = jnp.stack([number, row, jnp.ones_like(row)])[:, None, :]
    places = jnp.sum(jnp.where(to, columns, 0), axis=2)
    total = jnp.sum(chosen, dtype=jnp.int32)
    places = jnp.concatenate([places[:2], jnp.broadcast_to(total, (1, NS))])
    at = GROUPS * jnp.where(crowded, number, owner * ROOM + rank)
    return places, at, crowded


def share(places, received, blocks):
    rows = pick(places, received, blocks, ROOM, False)
    flat = rows.reshape(blocks, 1, ROOM * GROUPS * 128)
    return lax.all_to_all(flat, "rblk", split_axis=0, concat_axis=0, tiled=True).reshape(rows.shape)


def share_all(places, received, blocks):
    rows = pick(places, received, 1, NS, True)
    total = jnp.sum(lax.all_gather(rows, "rblk", axis=0, tiled=False), axis=0)
    return jnp.pad(total, ((0, (blocks * ROOM - NS) * GROUPS), (0, 0)))


def shards(records, source_index, band_edges):
    blocks = lax.axis_size("rblk")
    places, at, crowded = plan(source_index, lax.axis_index("rblk"))
    sent = spectra(jnp.transpose(records, (1, 0, 2)), band_edges)
    flat = sent.reshape(NDEV, 1, ROWS * 128)
    received = lax.all_to_all(flat, "chan", split_axis=0, concat_axis=0, tiled=True).reshape(sent.shape)
    sources = lax.cond(
        crowded,
        functools.partial(share_all, blocks=blocks),
        functools.partial(share, blocks=blocks),
        places,
        received,
    )
    return correlate(at, sources, received)


def solution(mesh):
    return jax.shard_map(
        shards,
        mesh=mesh,
        in_specs=(P(None, ("rblk", "chan"), None), P(), P()),
        out_specs=P("chan", None, None, "rblk"),
        check_vma=False,
    )
```

```python
import functools

import jax
import jax.numpy as jnp
import numpy as np
from jax import lax
from jax.experimental import pallas as pl
from jax.experimental.pallas import tpu as pltpu
from jax.sharding import PartitionSpec as P

SEG = 8
NSAMP = 7680
F_LOW = 7
NF = 1536
NB = 32
NS = 64
NDEV = 64
NBIN = 24
CH = 10
HOP = NSAMP // NBIN
HPAD = 384
GROUPS = 3
ROWS = GROUPS * CH
ROOM = 16
RECV = NDEV * CH

EPS = 1e-06
CLIP = 2.0
F32 = jnp.float32
BF16 = jnp.bfloat16
NT = (((1,), (1,)), ((), ()))
VMEM_LIMIT = 40 * 1024 * 1024
FULL_VMEM = 60 * 1024 * 1024


def split_np(values):
    hi = values.astype(jnp.bfloat16)
    lo = (values - hi.astype(np.float64)).astype(jnp.bfloat16)
    return hi, lo


@functools.lru_cache(maxsize=None)
def tables():
    m = np.arange(HPAD)
    s = np.arange(NBIN) + F_LOW
    angle = 2.0 * np.pi * ((s[:, None] * m[None, :]) % NSAMP) / NSAMP
    twiddle = np.stack([np.cos(angle), -np.sin(angle)], axis=1)
    d = np.arange(NDEV)
    angle = 2.0 * np.pi * ((m[:HOP, None] * d[None, :]) % HOP) / HOP
    cos, sin = np.cos(angle), np.sin(angle)
    of_re, of_im = np.concatenate([cos, -sin], axis=1), np.concatenate([sin, cos], axis=1)
    cuts = [slice(0, 128), slice(128, 256), slice(256, HOP)]
    w_hi, w_lo = split_np(np.concatenate([part[cut] for cut in cuts for part in (of_re, of_im)]))
    both = np.concatenate([w_hi, w_lo], axis=1)
    last = np.concatenate([w_hi[512:], np.zeros_like(w_lo[512:])], axis=1)
    return twiddle.reshape(2 * NBIN, HPAD).astype(np.float32), np.concatenate([both, last])


def split(x):
    hi = x.astype(BF16)
    lo = (x - hi.astype(F32)).astype(BF16)
    return hi, lo


def real_dft8(x):
    r = np.float32(np.sqrt(0.5))
    e0, e1, e2, e3 = x[0] + x[4], x[1] + x[5], x[2] + x[6], x[3] + x[7]
    f0, f1, f2, f3 = x[0] - x[4], x[1] - x[5], x[2] - x[6], x[3] - x[7]
    g0, g1 = e0 + e2, e1 + e3
    p, q = (f1 - f3) * r, (f1 + f3) * r
    return [
        (g0 + g1, None),
        (f0 + p, -(f2 + q)),
        (e0 - e2, e3 - e1),
        (f0 - p, f2 - q),
        (g0 - g1, None),
    ]


def real_dft24(x):
    h = np.float32(np.sqrt(3.0) / 2.0)
    parts = [real_dft8([x[(8 * a + 3 * b) % 24] for b in range(8)]) for a in range(3)]
    out = [None] * 24

    def put(ka, kb, re, im):
        k = (16 * ka + 9 * kb) % 24
        out[k] = (re, im)
        if (24 - k) % 24 != k:
            out[24 - k] = (re, None if im is None else -im)

    for kb in range(5):
        (r0, i0), (r1, i1), (r2, i2) = (parts[a][kb] for a in range(3))
        sr, dr = r1 + r2, (r1 - r2) * h
        cr = r0 - 0.5 * sr
        if i0 is None:
            put(0, kb, r0 + sr, None)
            put(1, kb, cr, -dr)
        else:
            si, di = i1 + i2, (i1 - i2) * h
            ci = i0 - 0.5 * si
            put(0, kb, r0 + sr, i0 + si)
            put(1, kb, cr + di, ci - dr)
            put(2, kb, cr - di, ci + dr)
    return out


def spectra_kernel(
    rec_hbm, edge_hbm, tw_hbm, w_hbm, out_ref,
    rec_ref, even_ref, odd_ref, z_ref, p_ref, m_ref, tw_ref, w_ref, edge_ref, rec_sems, sems,
):
    def fetch(i):
        return pltpu.make_async_copy(rec_hbm.at[i], rec_ref.at[i], rec_sems.at[i])

    small = [(edge_hbm, edge_ref), (tw_hbm, tw_ref), (w_hbm, w_ref)]
    edge_copy, tw_copy, w_copy = [pltpu.make_async_copy(a, b, sems.at[k]) for k, (a, b) in enumerate(small)]
    edge_copy.start()
    fetch(0).start()
    tw_copy.start()
    fetch(1).start()
    w_copy.start()
    for i in range(2, CH):
        fetch(i).start()

    edge_copy.wait()
    shape = (NB, 128)
    row = lax.broadcasted_iota(jnp.int32, shape, 0)
    low, high = jnp.zeros(shape, jnp.int32), jnp.zeros(shape, jnp.int32)
    for k in range(NB):
        low = jnp.where(row == k, edge_ref[k], low)
        high = jnp.where(row == k, edge_ref[k + 1], high)
    widths = (high - low).astype(F32)
    eye = row == lax.broadcasted_iota(jnp.int32, shape, 1)
    widths = jnp.sum(jnp.where(eye, widths, 0.0), axis=0, keepdims=True)[:, :NB]
    start = (lax.broadcasted_iota(jnp.int32, shape, 1) & (NDEV - 1)) * NBIN
    for s in range(NBIN):
        inside = (start + s >= low) & (start + s < high)
        m_ref[:, pl.ds(s * 128, 128)] = jnp.where(inside, 1.0, 0.0).astype(BF16)
    tw_copy.wait()

    lane = lax.broadcasted_iota(jnp.int32, (SEG, 128), 1)
    low_half = lane < 64

    def transform(i, a_ref):
        def tile(n):
            return rec_ref[i, :, pl.ds(n * 128, 128)].astype(F32)

        total = [None] * 4
        for n in range(NSAMP // 128):
            v = tile(n)
            total[n % 4] = v * v if total[n % 4] is None else total[n % 4] + v * v
        power = jnp.sum((total[0] + total[1]) + (total[2] + total[3]), axis=1, keepdims=True)
        bound = jnp.broadcast_to(CLIP * jnp.sqrt(power * (1.0 / NSAMP) + EPS), (SEG, 128))

        def clip(v):
            return jnp.minimum(jnp.maximum(v, -bound), bound)

        for q in range(3):
            x = []
            for a in range(NBIN):
                n = (a // 2) * 5 + q
                if a % 2 == 0:
                    x.append(clip(tile(n)))
                else:
                    left = tile(n + 2)
                    right = tile(n + 3) if q < 2 else left
                    x.append(clip(pltpu.roll(jnp.where(low_half, right, left), 64, 1)))
            y = real_dft24(x)
            for pair in range(NBIN // 2):
                res, ims = [], []
                for s in (2 * pair, 2 * pair + 1):
                    re, im = y[(s + F_LOW) % 24]
                    c = tw_ref[pl.ds(2 * s, 1), pl.ds(q * 128, 128)]
                    e = tw_ref[pl.ds(2 * s + 1, 1), pl.ds(q * 128, 128)]
                    if im is None:
                        res.append(re * c)
                        ims.append(re * e)
                    else:
                        res.append(re * c - im * e)
                        ims.append(re * e + im * c)
                rows = pl.ds(pair * 16, 16)
                if q == 2:
                    values = [jnp.where(low_half, r, pltpu.roll(i, 64, 1)) for r, i in zip(res, ims)]
                    hi, lo = split(jnp.concatenate(values, axis=0))
                    a_ref[4, rows, pl.ds(0, 128)] = hi
                    a_ref[4, rows, pl.ds(128, 128)] = lo
                    continue
                for part, values in enumerate((res, ims)):
                    hi, lo = split(jnp.concatenate(values, axis=0))
                    a_ref[q, rows, pl.ds(part * 128, 128)] = hi
                    a_ref[2 + q, rows, pl.ds(part * 128, 128)] = lo

    def multiply(i, a_ref):
        both = jnp.dot(a_ref[0], w_ref[pl.ds(0, 256), :], preferred_element_type=F32)
        both = both + jnp.dot(a_ref[1], w_ref[pl.ds(256, 256), :], preferred_element_type=F32)
        both = both + jnp.dot(a_ref[4], w_ref[pl.ds(512, 256), :], preferred_element_type=F32)
        rest = jnp.dot(a_ref[2], w_ref[pl.ds(0, 256), pl.ds(0, 128)], preferred_element_type=F32)
        rest = rest + jnp.dot(a_ref[3], w_ref[pl.ds(256, 256), pl.ds(0, 128)], preferred_element_type=F32)
        z = (both[:, :128] + both[:, 128:]) + rest
        z_ref[pl.ds(i * NBIN * SEG, NBIN * SEG), :] = z
        for s in range(NBIN):
            v = z[s * SEG : (s + 1) * SEG]
            p_ref[pl.ds(i * SEG, SEG), pl.ds(s * 128, 128)] = v * v

    half64 = lax.broadcasted_iota(jnp.int32, (64, 128), 1) < 64

    def whiten():
        rows = CH * SEG
        member = m_ref[...]
        power = jnp.concatenate(split(p_ref[...]), axis=0)
        band = lax.dot_general(power, member, NT, preferred_element_type=F32)
        scale = lax.rsqrt((band[:rows] + band[rows:]) / widths + EPS)
        s_hi = scale.astype(BF16)
        s_mid, s_lo = split(scale - s_hi.astype(F32))
        scales = jnp.concatenate([s_hi, s_mid, s_lo], axis=1)
        copied = jnp.concatenate([member] * 3, axis=0)
        p_ref[...] = jnp.dot(scales, copied, preferred_element_type=F32)

    def whitened(t, i):
        z = z_ref[pl.ds(i * NBIN * SEG + t * 64, 64), :]
        factor = [p_ref[pl.ds(i * SEG, SEG), pl.ds((t * 8 + u) * 128, 128)] for u in range(8)]
        return z * jnp.concatenate(factor, axis=0)

    def place(*pair):
        first, second = (whitened(t, i) for t, i in pair)
        upper = jnp.where(half64, first, pltpu.roll(second, 64, 1))
        lower = jnp.where(half64, pltpu.roll(first, 64, 1), second)
        halves = [h[u * SEG : (u + 1) * SEG] for u in range(8) for h in (upper, lower)]
        turned = jnp.concatenate(halves, axis=0).T
        for part, (t, i) in enumerate(pair):
            out_ref[pl.ds(t * CH + i, NDEV, stride=ROWS), :] = turned[part * 64 : part * 64 + 64]

    a_refs = (even_ref, odd_ref)
    for i in range(CH):
        fetch(i).wait()
        if i:
            multiply(i - 1, a_refs[(i - 1) % 2])
        transform(i, a_refs[i % 2])
        if i == 0:
            w_copy.wait()
    multiply(CH - 1, a_refs[(CH - 1) % 2])
    whiten()
    for i in range(0, CH, 2):
        for t in range(GROUPS):
            place((t, i), (t, i + 1))


def vmem():
    return pl.BlockSpec(memory_space=pltpu.VMEM)


def smem():
    return pl.BlockSpec(memory_space=pltpu.SMEM)


def spectra(records, band_edges):
    twiddle, w = tables()
    return pl.pallas_call(
        spectra_kernel,
        out_shape=jax.ShapeDtypeStruct((NDEV * ROWS, 128), F32),
        in_specs=[pl.BlockSpec(memory_space=pltpu.HBM)] * 4,
        out_specs=vmem(),
        scratch_shapes=[
            pltpu.VMEM((CH, SEG, NSAMP), BF16),
            pltpu.VMEM((5, NBIN * SEG, 256), BF16),
            pltpu.VMEM((5, NBIN * SEG, 256), BF16),
            pltpu.VMEM((CH * NBIN * SEG, 128), F32),
            pltpu.VMEM((CH * SEG, NBIN * 128), F32),
            pltpu.VMEM((NB, NBIN * 128), BF16),
            pltpu.VMEM(twiddle.shape, F32),
            pltpu.VMEM(w.shape, BF16),
            pltpu.SMEM((NB + 1,), jnp.int32),
            pltpu.SemaphoreType.DMA((CH,)),
            pltpu.SemaphoreType.DMA((3,)),
        ],
        compiler_params=pltpu.CompilerParams(vmem_limit_bytes=FULL_VMEM),
        name="spectra",
    )(records, band_edges, jnp.asarray(twiddle), jnp.asarray(w))


def pick_kernel(copies, rows, ordered, place_ref, recv_ref, out_ref, held_ref):
    held_ref[...] = jnp.zeros_like(held_ref)

    def one(n, carry):
        to = place_ref[0, n] if ordered else n
        held_ref[pl.ds(to * GROUPS, GROUPS), :] = recv_ref[pl.ds(place_ref[1, n], GROUPS, stride=CH), :]
        return carry

    lax.fori_loop(0, place_ref[2, 0], one, 0)
    for k in range(copies):
        out_ref[pl.ds(k * rows, rows), :] = held_ref[...]


def pick(places, received, copies, room, ordered):
    rows = room * GROUPS
    return pl.pallas_call(
        functools.partial(pick_kernel, copies, rows, ordered),
        out_shape=jax.ShapeDtypeStruct((copies * rows, 128), F32),
        in_specs=[smem(), vmem()],
        out_specs=vmem(),
        scratch_shapes=[pltpu.VMEM((rows, 128), F32)],
        compiler_params=pltpu.CompilerParams(vmem_limit_bytes=VMEM_LIMIT),
        name="pick",
    )(places, received)


def correlate_kernel(chosen_ref, src_ref, recv_ref, out_hbm, left_ref, right_ref, dense_ref, out_ref, sems):
    places = chosen_ref.shape[1]
    lower = lax.broadcasted_iota(jnp.int32, (RECV, 128), 1) < 64
    lane = lax.broadcasted_iota(jnp.int32, (2 * NS, 128), 1)
    imag = lane[:NS] & SEG != 0
    which = lane // (2 * SEG)
    sources = []
    for t in range(GROUPS):
        parts = jnp.concatenate(split(src_ref[pl.ds(t, places, stride=GROUPS), :] * (1.0 / SEG)), axis=1)
        s = jnp.dot(chosen_ref[...], parts, preferred_element_type=F32)
        hi, lo = (
            jnp.concatenate([v, jnp.where(imag, pltpu.roll(v, SEG, 1), -pltpu.roll(v, 128 - SEG, 1))], axis=0)
            for v in (s[:, :128], s[:, 128:])
        )
        sources.append((hi, lo))
    copies = []
    for t in range(GROUPS):
        for i in range(CH):
            dense_ref[t, pl.ds(i, NDEV, stride=CH), :] = recv_ref[pl.ds(t * CH + i, NDEV, stride=ROWS), :]

        hi, lo = split(dense_ref[t])
        turned = pltpu.roll(lo.astype(F32), 64, 1).astype(BF16)
        right_ref[t, 0] = jnp.where(lower, hi, turned)
        right_ref[t, 1] = jnp.where(lower, turned, hi)
        right_ref[t, 2] = hi

        hi, lo = sources[t]
        hi_turned = pltpu.roll(hi, 64, 1)
        for h in range(2):
            part = 2 * t + h
            both = jnp.where((lane < 64) == (h == 0), hi, hi_turned)
            for v in range(4):
                rows = pl.ds(v * 2 * NS, 2 * NS)
                left_ref[part, rows, pl.ds(0, 128)] = jnp.where(which % 4 == v, both, 0.0).astype(BF16)
                left_ref[part, rows, pl.ds(128, 128)] = jnp.where(which == 4 * h + v, lo, 0.0).astype(BF16)
            right = jnp.concatenate([right_ref[t, h], right_ref[t, 2]], axis=1)
            for w in range(2):
                left = left_ref[part, pl.ds(w * 4 * NS, 4 * NS)]
                result = lax.dot_general(left, right, NT, preferred_element_type=F32)
                piece = 2 * part + w
                bins = pl.ds(2 * piece, 2)
                out_ref[bins] = result.astype(BF16).reshape(2, 2, NS, RECV)
                copies.append(pltpu.make_async_copy(out_ref.at[bins], out_hbm.at[bins], sems.at[piece]))
                copies[-1].start()
    for copy in copies:
        copy.wait()


def correlate(chosen, sources, received):
    parts = 2 * GROUPS
    return pl.pallas_call(
        correlate_kernel,
        out_shape=jax.ShapeDtypeStruct((NBIN, 2, NS, RECV), BF16),
        in_specs=[vmem()] * 3,
        out_specs=pl.BlockSpec(memory_space=pltpu.HBM),
        scratch_shapes=[
            pltpu.VMEM((parts, 8 * NS, 256), BF16),
            pltpu.VMEM((GROUPS, 3, RECV, 128), BF16),
            pltpu.VMEM((GROUPS, RECV, 128), F32),
            pltpu.VMEM((NBIN, 2, NS, RECV), BF16),
            pltpu.SemaphoreType.DMA((2 * parts,)),
        ],
        compiler_params=pltpu.CompilerParams(vmem_limit_bytes=VMEM_LIMIT),
        name="correlate",
    )(chosen, sources, received)


def plan(source_index, block, blocks):
    owner, local = source_index // RECV, source_index % RECV
    number = jnp.arange(NS, dtype=jnp.int32)
    same = owner[:, None] == owner[None, :]
    rank = jnp.sum(same & (number[None, :] < number[:, None]), axis=1, dtype=jnp.int32)
    crowded = jnp.any(rank >= ROOM)
    chosen = owner == block
    to = (chosen & (rank == number[:, None]))[None]
    row = local // CH * ROWS + local % CH
    columns = jnp.stack([number, row, jnp.ones_like(row)])[:, None, :]
    places = jnp.sum(jnp.where(to, columns, 0), axis=2)
    total = jnp.sum(chosen, dtype=jnp.int32)
    places = jnp.concatenate([places[:2], jnp.broadcast_to(total, (1, NS))])
    at = jnp.where(crowded, number, owner * ROOM + rank)
    moved = at[:, None] == jnp.arange(blocks * ROOM, dtype=jnp.int32)[None, :]
    return places, moved.astype(F32).astype(BF16), crowded


def share(places, received, blocks):
    rows = pick(places, received, blocks, ROOM, False)
    flat = rows.reshape(blocks, 1, ROOM * GROUPS * 128)
    return lax.all_to_all(flat, "rblk", split_axis=0, concat_axis=0, tiled=True).reshape(rows.shape)


def share_all(places, received, blocks):
    rows = pick(places, received, 1, NS, True)
    total = jnp.sum(lax.all_gather(rows, "rblk", axis=0, tiled=False), axis=0)
    return jnp.pad(total, ((0, (blocks * ROOM - NS) * GROUPS), (0, 0)))


def shards(records, source_index, band_edges):
    blocks = lax.axis_size("rblk")
    places, chosen, crowded = plan(source_index, lax.axis_index("rblk"), blocks)
    sent = spectra(jnp.transpose(records, (1, 0, 2)), band_edges)
    flat = sent.reshape(NDEV, 1, ROWS * 128)
    received = lax.all_to_all(flat, "chan", split_axis=0, concat_axis=0, tiled=True).reshape(sent.shape)
    sources = lax.cond(
        crowded,
        functools.partial(share_all, blocks=blocks),
        functools.partial(share, blocks=blocks),
        places,
        received,
    )
    return correlate(chosen, sources, received)


def solution(mesh):
    return jax.shard_map(
        shards,
        mesh=mesh,
        in_specs=(P(None, ("rblk", "chan"), None), P(), P()),
        out_specs=P("chan", None, None, "rblk"),
        check_vma=False,
    )
```
